32 devices in a mesh: coarse: 8 (over y, x, core), fan: 4 (over z).
Axes of the slice: x: 2, y: 2, z: 4, core: 2. Of those that a mesh axis runs over, the one named last changes fastest.
Arguments:
- right_side: float32 [512, 64, 128], P(('coarse', 'fan')), may hold values from -6 to 6
- fine_matrix: bfloat16 [512, 7, 64, 64], P(('coarse', 'fan')), as said below
- fine_columns: int32 [512, 7], P(('coarse', 'fan')), may hold values from 0 to 23, as said below
- fine_inverse: bfloat16 [512, 64, 64], P(('coarse', 'fan')), as said below
- prolong: bfloat16 [512, 64, 64], P(('coarse', 'fan')), may hold values from -0.75 to 0.75
- aggregate: int32 [512], P(('coarse', 'fan')), may hold values from 0 to 1, as said below
- coarse_matrix: bfloat16 [64, 7, 64, 64], P('coarse'), as said below
- coarse_columns: int32 [64, 7], P('coarse'), may hold values from 0 to 11, as said below
- coarse_inverse: bfloat16 [64, 64, 64], P('coarse'), as said below
Outputs:
- solution: float32 [512, 64, 128], P(('coarse', 'fan'))
- residual_out: float32 [512, 64, 128], P(('coarse', 'fan'))
The draws below stay inside these ranges and needn't reach their ends.
Inputs may be any that keep to these rules, and one draw needn't show every extreme that they name: `fine_columns`: slot 0 names the row itself; every entry lies within 4 of the row's own position plus 4. `coarse_columns`: slot 0 names the row itself. `aggregate`: every value is named by exactly 8 rows of each device. `fine_matrix`: slot 0 is the diagonal block. `coarse_matrix`: slot 0 is the diagonal block. `fine_inverse`: approximates the inverse of the fine diagonal block. `coarse_inverse`: approximates the inverse of the coarse diagonal block.
All inputs are finite; a program needn't handle non-finite values.
Results may differ from the reference program's by a relative error of at most 0.02.
Values sent between devices are 32-bit elements; how exact they have to be, the bound alone decides.
A program may use at most 64 MiB of HBM per device.

```python
import math
import jax
import jax.numpy as jnp
from jax import lax

B = 64
R = 128
RB = 16
K = 7
KC = 7
H = 4
HC = 2
CYCLES = 2
SWEEPS = 2
CSWEEPS = 4
RC = 2
GROUP = 8
NF = 512
NC = 64


def operator_parts(key, rows, slots, salt, log_low, log_high, outer_scale):
    scale_key, inner_key, outer_key = jax.random.split(jax.random.fold_in(key, salt), 3)
    logs = jax.random.uniform(scale_key, (rows, B), jnp.float32, math.log(log_low), math.log(log_high))
    diagonal = jnp.exp(logs)
    inner = jax.random.normal(inner_key, (rows, B, B), jnp.float32)
    outer = jax.random.normal(outer_key, (rows, slots - 1, B, B), jnp.float32)
    identity = jnp.eye(B, dtype=jnp.float32)
    inner = inner * (0.3 / math.sqrt(B)) * (1.0 - identity)
    outer = outer * (outer_scale / math.sqrt(B))
    return (diagonal, inner, outer, identity)


def assemble_matrix(key, rows, slots, salt, log_low, log_high, outer_scale):
    diagonal, inner, outer, identity = operator_parts(key, rows, slots, salt, log_low, log_high, outer_scale)
    head = inner + identity[None, :, :] * diagonal[:, :, None]
    return jnp.concatenate([head[:, None], outer], 1).astype(jnp.bfloat16)


def assemble_inverse(key, rows, slots, salt, log_low, log_high, outer_scale):
    diagonal, inner, outer, identity = operator_parts(key, rows, slots, salt, log_low, log_high, outer_scale)
    recip = 1.0 / diagonal
    result = identity[None, :, :] * recip[:, :, None] - inner * recip[:, :, None] * recip[:, None, :]
    return result.astype(jnp.bfloat16)


def column_draw(key, rows, group, slots, reach):
    sign_key, size_key, first_key = jax.random.split(jax.random.fold_in(key, 3), 3)
    position = jnp.arange(rows, dtype=jnp.int32) % group
    first_sign = jax.random.randint(first_key, (rows,), 0, 2) * 2 - 1
    first_sign = jnp.where(position == 0, -1, jnp.where(position == group - 1, 1, first_sign))
    signs = jax.random.randint(sign_key, (rows, slots - 2), 0, 2) * 2 - 1
    widths = jax.random.randint(size_key, (rows, slots - 2), 1, reach + 1)
    offsets = jnp.concatenate([jnp.zeros((rows, 1), jnp.int32), (first_sign * reach)[:, None], signs * widths], 1)
    return (reach + position[:, None] + offsets).astype(jnp.int32)


def coarse_column_draw(key, rows, group, slots, reach):
    rim_key, any_key = jax.random.split(jax.random.fold_in(key, 5), 2)
    position = jnp.arange(rows, dtype=jnp.int32) % group
    rim_pick = jax.random.randint(rim_key, (rows,), 0, 2 * reach)
    rim_column = jnp.where(rim_pick < reach, rim_pick, group + rim_pick)
    others = jax.random.randint(any_key, (rows, slots - 2), 0, group + 2 * reach)
    return jnp.concatenate([(reach + position)[:, None], rim_column[:, None], others], 1).astype(jnp.int32)


def draw_fine_matrix(key, part):
    return assemble_matrix(key, NF, K, 7, 1.5, 6.0, 0.35)


def draw_fine_inverse(key, part):
    return assemble_inverse(key, NF, K, 7, 1.5, 6.0, 0.35)


def draw_coarse_matrix(key, part):
    return assemble_matrix(key, NC, KC, 11, 1.2, 3.0, 0.5)


def draw_coarse_inverse(key, part):
    return assemble_inverse(key, NC, KC, 11, 1.2, 3.0, 0.5)


def draw_fine_columns(key, part):
    return column_draw(key, NF, RB, K, H)


def draw_coarse_columns(key, part):
    return coarse_column_draw(key, NC, GROUP, KC, HC)


def draw_aggregate(key, part):
    keys = jax.random.split(key, NF // RB)
    orders = jax.vmap(lambda single: jax.random.permutation(single, RB))(keys)
    return (orders % RC).reshape(NF).astype(jnp.int32)


def steps_of(own_key, dims, cuts, least, top_value):
    def one(dim, parts):
        heights = jax.random.uniform(jax.random.fold_in(jax.random.fold_in(own_key, 6), dim), (parts,), jnp.float32, least / len(cuts), top_value / len(cuts))
        return jnp.repeat(jnp.exp(heights), dims[dim] // parts).reshape((-1,) + (1,) * (len(dims) - dim - 1))

    factor_of = one(*cuts[0])
    for cut in cuts[1:]:
        factor_of = factor_of * one(*cut)
    return factor_of


def centred(own_key, extent, spread, most, cuts=(), kind=jnp.bfloat16):
    values = jax.random.normal(own_key, extent, jnp.float32) * spread
    if len(cuts) > 0:
        values = steps_of(own_key, extent, cuts, -0.22, 0.18) * values
    return jnp.clip(values, min=-most, max=most).astype(kind)


def setup_inputs(seed: int = 0) -> dict:
    seeds = jax.random.split(jax.random.key(seed), 10)
    return {
        "right_side": centred(seeds[0], (NF, B, R), 1.0, 6.0, ((0, 32),), jnp.float32),
        "fine_matrix": draw_fine_matrix(jax.random.fold_in(seeds[9], 71), 0),
        "fine_columns": draw_fine_columns(jax.random.fold_in(seeds[9], 71), 0),
        "fine_inverse": draw_fine_inverse(jax.random.fold_in(seeds[9], 71), 0),
        "prolong": centred(seeds[4], (NF, B, B), B ** -0.5, 0.75, ((0, 32),)),
        "aggregate": draw_aggregate(jax.random.fold_in(seeds[9], 71), 0),
        "coarse_matrix": draw_coarse_matrix(jax.random.fold_in(seeds[9], 71), 0),
        "coarse_columns": draw_coarse_columns(jax.random.fold_in(seeds[9], 71), 0),
        "coarse_inverse": draw_coarse_inverse(jax.random.fold_in(seeds[9], 71), 0),
    }


relaxation = 0.6


def block_product(matrix, columns, vector_in, group, reach):
    total = vector_in.shape[0]
    groups = total // group
    padded = jnp.pad(vector_in, ((reach, reach), (0, 0), (0, 0)))
    shaped_matrix = matrix.reshape((groups, group) + matrix.shape[1:])
    shaped_columns = columns.reshape(groups, group, columns.shape[1])

    def per_group(pieces):
        group_index, group_matrix, group_columns = pieces
        window = lax.dynamic_slice_in_dim(padded, group_index * group, group + 2 * reach, 0)
        picked = window[group_columns]
        return jnp.einsum("rkij,rkjs->ris", group_matrix.astype(jnp.float32), picked.astype(jnp.float32), precision=lax.Precision.HIGHEST)

    result = lax.map(per_group, (jnp.arange(groups, dtype=jnp.int32), shaped_matrix, shaped_columns))
    return result.reshape(vector_in.shape)


def relax_inverse(inverse, residual_in):
    rounded = lax.optimization_barrier(residual_in.astype(jnp.bfloat16))
    return relaxation * jnp.einsum("nij,njs->nis", inverse.astype(jnp.float32), rounded.astype(jnp.float32), precision=lax.Precision.HIGHEST)


def reference(right_side, fine_matrix, fine_columns, fine_inverse, prolong, aggregate, coarse_matrix, coarse_columns, coarse_inverse):
    fine_total = right_side.shape[0]
    parent = (jnp.arange(fine_total, dtype=jnp.int32) // RB) * RC + aggregate

    def fine_apply(vector_in):
        return block_product(fine_matrix, fine_columns, vector_in, RB, H)

    def coarse_apply(vector_in):
        return block_product(coarse_matrix, coarse_columns, vector_in, GROUP, HC)

    def smooth(solution_now):
        if solution_now is None:
            return relax_inverse(fine_inverse, right_side)
        return solution_now + relax_inverse(fine_inverse, right_side - fine_apply(solution_now))

    solution = None
    for cycle_index in range(CYCLES):
        for sweep_index in range(SWEEPS):
            solution = smooth(solution)
        residual_now = right_side - fine_apply(solution)
        rounded = lax.optimization_barrier(residual_now.astype(jnp.bfloat16))
        terms = jnp.einsum("nji,njs->nis", prolong.astype(jnp.float32), rounded.astype(jnp.float32), precision=lax.Precision.HIGHEST)
        coarse_rhs = jax.ops.segment_sum(terms, parent, num_segments=NC)
        correction = relax_inverse(coarse_inverse, coarse_rhs)
        for sweep_index in range(CSWEEPS - 1):
            correction = correction + relax_inverse(coarse_inverse, coarse_rhs - coarse_apply(correction))
        lifted = correction[parent]
        solution = solution + jnp.einsum("nij,njs->nis", prolong.astype(jnp.float32), lifted, precision=lax.Precision.HIGHEST)
        for sweep_index in range(SWEEPS):
            solution = smooth(solution)
    residual_out = right_side - fine_apply(solution)
    return solution, residual_out
```

```python
import functools

import jax
import jax.numpy as jnp
from jax import lax
from jax.experimental import pallas as pl
from jax.experimental.pallas import tpu as pltpu
from jax.sharding import PartitionSpec as P

H = 4
HC = 2
CSWEEPS = 4
EXCHANGES = 8
relaxation = 0.6
MESH = pl.DeviceIdType.MESH
F32 = jnp.float32
BF16 = jnp.bfloat16


def dot(a, b):
    return jnp.dot(a, b, preferred_element_type=F32)


def two_term(matrix, halves):
    both = dot(matrix, halves)
    width = both.shape[1] // 2
    return both[:, :width] + both[:, width:]


def kernel(
    coarse_size, fan_size,
    b_ref, a_ref, acol_ref, d_ref, p_ref, agg_ref, c_ref, ccol_ref, ci_ref,
    x_ref, res_ref,
    ad, dd, pd, ptd, cd, cid, xhl, ehl, e_ref, rhs, edge_out, halo_in,
    ce_out, ce_in, pe_out, pe_in,
    fs_sem, fr_sem, gs_sem, gr_sem, cs_sem, cr_sem, ps_sem, pr_sem,
):
    rows, slots, B, _ = a_ref.shape
    R = b_ref.shape[1]
    grows = c_ref.shape[0]
    rc = grows // fan_size
    HB = H * B
    CB = HC * B
    PB = rc * B
    ng = rows // H
    c = lax.axis_index("coarse")
    f = lax.axis_index("fan")
    place = c * fan_size + f
    before, after = place - 1, place + 1
    fine_to = (
        (before // fan_size, before % fan_size),
        (after // fan_size, after % fan_size),
    )
    fine_has = (place > 0, place < coarse_size * fan_size - 1)
    coarse_to = ((c - 1, f), (c + 1, f))
    coarse_has = (c > 0, c < coarse_size - 1)
    peers = [(c, (f + k) % fan_size) for k in range(1, fan_size)]

    barrier = pltpu.get_barrier_semaphore()
    for has, to in zip(fine_has + coarse_has, fine_to + coarse_to):
        @pl.when(has)
        def _():
            pl.semaphore_signal(barrier, inc=1, device_id=to, device_id_type=MESH)
    for to in peers:
        pl.semaphore_signal(barrier, inc=1, device_id=to, device_id_type=MESH)

    half = (lax.broadcasted_iota(jnp.int32, (1, 2 * B), 1) >= B).astype(jnp.int32)

    def build(count, blocks, names, pairs, dst):
        def row(r, carry):
            doubled = []
            for block in blocks(r):
                wide = block.astype(F32)
                doubled.append(jnp.concatenate([wide, wide], axis=1))
            named = names(r)
            for p in range(pairs):
                at = half + 2 * p
                total = None
                for block, name in zip(doubled, named):
                    term = jnp.where(at == name, block, 0.0)
                    total = term if total is None else total + term
                dst[pl.ds(pl.multiple_of(r * B, B), B), 2 * p * B:(2 * p + 2) * B] = total.astype(BF16)
            return carry

        lax.fori_loop(0, count, row, 0)

    def put_halves(ref, start, value):
        high = value.astype(BF16)
        low = (value - high.astype(F32)).astype(BF16)
        n = value.shape[0]
        ref[start:start + n, :R] = high
        ref[start:start + n, R:] = low

    def fine_copy(t, d):
        return pltpu.make_async_remote_copy(
            src_ref=edge_out.at[t, d], dst_ref=halo_in.at[t, 1 - d],
            send_sem=fs_sem.at[t, d], recv_sem=fr_sem.at[t, 1 - d],
            device_id=fine_to[d], device_id_type=MESH)

    def fine_send(t, d, value):
        edge_out[t, d] = value

        @pl.when(fine_has[d])
        def _():
            fine_copy(t, d).start()

    def fine_wait(t, d, slot):
        @pl.when(fine_has[d])
        def _():
            pltpu.make_async_remote_copy(
                src_ref=edge_out.at[t, 1 - d], dst_ref=halo_in.at[t, d],
                send_sem=fs_sem.at[t, 1 - d], recv_sem=fr_sem.at[t, d],
                device_id=fine_to[d], device_id_type=MESH).wait_recv()
            put_halves(xhl.at[slot], d * (rows + H) * B, halo_in[t, d])

    def coarse_copy(s, d):
        return pltpu.make_async_remote_copy(
            src_ref=ce_out.at[s, d], dst_ref=ce_in.at[s, 1 - d],
            send_sem=cs_sem.at[s, d], recv_sem=cr_sem.at[s, 1 - d],
            device_id=coarse_to[d], device_id_type=MESH)

    def coarse_sent(d, last):
        if not last:
            return coarse_has[d]
        return coarse_has[d] & (f == (fan_size - 1 if d == 0 else 0))

    def coarse_came(d, last):
        if not last:
            return coarse_has[d]
        return coarse_has[d] & (f == (0 if d == 0 else fan_size - 1))

    def coarse_send(s, d, value, last):
        ce_out[s, d] = value

        @pl.when(coarse_sent(d, last))
        def _():
            coarse_copy(s, d).start()

    def coarse_wait(s, d, last):
        @pl.when(coarse_came(d, last))
        def _():
            pltpu.make_async_remote_copy(
                src_ref=ce_out.at[s, 1 - d], dst_ref=ce_in.at[s, d],
                send_sem=cs_sem.at[s, 1 - d], recv_sem=cr_sem.at[s, d],
                device_id=coarse_to[d], device_id_type=MESH).wait_recv()
            put_halves(ehl, d * (grows + HC) * B, ce_in[s, d])

    def edge_matrix_copy(d):
        return pltpu.make_async_remote_copy(
            src_ref=pe_out.at[d], dst_ref=pe_in.at[1 - d],
            send_sem=ps_sem.at[d], recv_sem=pr_sem.at[1 - d],
            device_id=fine_to[d], device_id_type=MESH)

    def group(g):
        return slice(g * HB, (g + 1) * HB)

    def step_of(g, residual):
        return relaxation * dot(dd[group(g), :], residual.astype(BF16))

    def set_group(g, value, slot, t):
        x_ref[group(g), :] = value
        put_halves(xhl.at[slot], (g + 1) * HB, value)
        if t is not None and g == 0:
            fine_send(t, 0, value)
        if t is not None and g == ng - 1:
            fine_send(t, 1, value)

    def residuals(slot, t, use):
        for g in range(1, ng - 1):
            use(g, b_ref[group(g), :] - two_term(ad[group(g), :], xhl[slot, g * HB:(g + 3) * HB, :]))
        low = b_ref[group(0), :] - two_term(ad[group(0), HB:], xhl[slot, HB:3 * HB, :])
        last = ng - 1
        high = b_ref[group(last), :] - two_term(
            ad[group(last), :2 * HB], xhl[slot, last * HB:(last + 2) * HB, :])
        if t is not None:
            fine_wait(t, 0, slot)
        use(0, low - two_term(ad[group(0), :HB], xhl[slot, :HB, :]))
        if t is not None:
            fine_wait(t, 1, slot)
        use(last, high - two_term(ad[group(last), 2 * HB:], xhl[slot, (last + 2) * HB:, :]))

    def sweep(slot, t_in, t_out):
        def use(g, residual):
            set_group(g, x_ref[group(g), :] + step_of(g, residual), 1 - slot, t_out)

        residuals(slot, t_in, use)
        return 1 - slot

    def relax_coarse(values):
        return [
            relaxation * dot(cid[g * HB:(g + 1) * HB, :], v.astype(BF16))
            for g, v in enumerate(values)
        ]

    cg = grows // H

    def correct(cycle, slot, t_in):
        pieces = []

        def use(g, residual):
            pieces.append(dot(ptd[:, group(g)], residual.astype(BF16)))

        residuals(slot, t_in, use)
        mine = pl.ds(pl.multiple_of(f * PB, PB), PB)
        rhs[cycle, mine, :] = functools.reduce(jnp.add, pieces)
        copies = []
        for k, to in enumerate(peers):
            copy = pltpu.make_async_remote_copy(
                src_ref=rhs.at[cycle, mine], dst_ref=rhs.at[cycle, mine],
                send_sem=gs_sem.at[cycle, k], recv_sem=gr_sem.at[cycle, k],
                device_id=to, device_id_type=MESH)
            copy.start()
            copies.append(copy)
        if cycle == 0:
            pe_out[0] = pd[:HB, :].astype(F32)
            pe_out[1] = pd[(ng - 1) * HB:, :].astype(F32)
            for d in range(2):
                @pl.when(fine_has[d])
                def _():
                    edge_matrix_copy(d).start()
        for k in range(fan_size - 1):
            theirs = pl.ds(pl.multiple_of(((f - k - 1 + fan_size) % fan_size) * PB, PB), PB)
            pltpu.make_async_remote_copy(
                src_ref=rhs.at[cycle, theirs], dst_ref=rhs.at[cycle, theirs],
                send_sem=gs_sem.at[cycle, k], recv_sem=gr_sem.at[cycle, k],
                device_id=peers[k], device_id_type=MESH).wait_recv()

        def publish(e, s, last):
            coarse_send(s, 0, e[0][:CB, :], last)
            coarse_send(s, 1, e[-1][HB - CB:, :], last)
            for g in range(cg):
                e_ref[group(g), :] = e[g]
                put_halves(ehl, CB + g * HB, e[g])

        s = cycle * CSWEEPS
        publish(relax_coarse([rhs[cycle, group(g), :] for g in range(cg)]), s, False)
        for step in range(1, CSWEEPS):
            own = [
                rhs[cycle, group(g), :]
                - two_term(cd[group(g), CB:CB + grows * B], ehl[CB:CB + grows * B, :])
                for g in range(cg)
            ]
            coarse_wait(s, 0, False)
            own = [v - two_term(cd[group(g), :CB], ehl[:CB, :]) for g, v in enumerate(own)]
            coarse_wait(s, 1, False)
            own = [
                v - two_term(cd[group(g), CB + grows * B:], ehl[CB + grows * B:, :])
                for g, v in enumerate(own)
            ]
            e = [e_ref[group(g), :] + v for g, v in enumerate(relax_coarse(own))]
            s = s + 1
            publish(e, s, step == CSWEEPS - 1)

        other = 1 - slot
        lifted = ehl[pl.ds(pl.multiple_of(CB + f * PB, PB), PB), :]
        for g in range(ng):
            set_group(g, x_ref[group(g), :] + two_term(pd[group(g), :], lifted), other, None)
        for d in range(2):
            if cycle == 0:
                @pl.when(fine_has[d])
                def _():
                    pltpu.make_async_remote_copy(
                        src_ref=pe_out.at[1 - d], dst_ref=pe_in.at[d],
                        send_sem=ps_sem.at[1 - d], recv_sem=pr_sem.at[d],
                        device_id=fine_to[d], device_id_type=MESH).wait_recv()
            coarse_wait(s, d, True)

            @pl.when(fine_has[d])
            def _():
                theirs = ehl[pl.ds(pl.multiple_of(CB + (f + 2 * d - 1) * PB, PB), PB), :]
                value = halo_in[t_in, d] + two_term(pe_in[d].astype(BF16), theirs)
                put_halves(xhl.at[other], d * (rows + H) * B, value)
        return other, copies

    build(rows, lambda r: [d_ref[r]], lambda r: [r % H], H // 2, dd)
    waits = (
        sum(h.astype(jnp.int32) for h in fine_has + coarse_has) + (fan_size - 1)
    )
    pl.semaphore_wait(barrier, waits)
    for g in (0, ng - 1) + tuple(range(1, ng - 1)):
        set_group(g, step_of(g, b_ref[group(g), :]), 0, 0)
    for d in range(2):
        @pl.when(jnp.logical_not(fine_has[d]))
        def _():
            for slot in range(2):
                at = d * (rows + H) * B
                xhl[slot, at:at + HB, :] = jnp.zeros((HB, 2 * R), BF16)

        @pl.when(jnp.logical_not(coarse_has[d]))
        def _():
            at = d * (grows + HC) * B
            ehl[at:at + CB, :] = jnp.zeros((CB, 2 * R), BF16)

    build(
        rows,
        lambda r: [a_ref[r, k] for k in range(slots)],
        lambda r: [acol_ref[r, k] - (r // H) * H for k in range(slots)],
        3 * H // 2, ad)
    build(rows, lambda r: [p_ref[r]], lambda r: [agg_ref[r]], rc // 2, pd)
    for g in range(ng):
        ptd[:, group(g)] = jnp.transpose(pd[group(g), :].astype(F32)).astype(BF16)
    build(
        grows,
        lambda r: [c_ref[r, k] for k in range(c_ref.shape[1])],
        lambda r: [ccol_ref[r, k] for k in range(c_ref.shape[1])],
        (grows + 2 * HC) // 2, cd)
    build(grows, lambda r: [ci_ref[r]], lambda r: [r % H], H // 2, cid)

    slot = sweep(0, 0, 1)
    slot, first = correct(0, slot, 1)
    slot = sweep(slot, None, 2)
    slot = sweep(slot, 2, 3)
    slot = sweep(slot, 3, 4)
    slot = sweep(slot, 4, 5)
    slot, second = correct(1, slot, 5)
    slot = sweep(slot, None, 6)
    slot = sweep(slot, 6, 7)

    def keep(g, residual):
        res_ref[group(g), :] = residual

    residuals(slot, 7, keep)

    for copy in first + second:
        copy.wait_send()
    for d in range(2):
        @pl.when(fine_has[d])
        def _():
            for t in range(EXCHANGES):
                fine_copy(t, d).wait_send()
            edge_matrix_copy(d).wait_send()

        for s in range(2 * CSWEEPS):
            @pl.when(coarse_sent(d, s % CSWEEPS == CSWEEPS - 1))
            def _():
                coarse_copy(s, d).wait_send()


def body(coarse_size, fan_size, right_side, fine_matrix, fine_columns, fine_inverse,
         prolong, aggregate, coarse_matrix, coarse_columns, coarse_inverse):
    rows, B, R = right_side.shape
    grows = coarse_matrix.shape[0]
    rc = grows // fan_size
    vmem = pl.BlockSpec(memory_space=pltpu.VMEM)
    smem = pl.BlockSpec(memory_space=pltpu.SMEM)
    flat = jax.ShapeDtypeStruct((rows * B, R), F32)
    dma = pltpu.SemaphoreType.DMA
    solution_out, residual_out = pl.pallas_call(
        functools.partial(kernel, coarse_size, fan_size),
        out_shape=(flat, flat),
        in_specs=[vmem, vmem, smem, vmem, vmem, smem, vmem, smem, vmem],
        out_specs=(vmem, vmem),
        scratch_shapes=[
            pltpu.VMEM((rows * B, 3 * H * B), BF16),
            pltpu.VMEM((rows * B, H * B), BF16),
            pltpu.VMEM((rows * B, rc * B), BF16),
            pltpu.VMEM((rc * B, rows * B), BF16),
            pltpu.VMEM((grows * B, (grows + 2 * HC) * B), BF16),
            pltpu.VMEM((grows * B, H * B), BF16),
            pltpu.VMEM((2, (rows + 2 * H) * B, 2 * R), BF16),
            pltpu.VMEM(((grows + 2 * HC) * B, 2 * R), BF16),
            pltpu.VMEM((grows * B, R), F32),
            pltpu.VMEM((2, grows * B, R), F32),
            pltpu.VMEM((EXCHANGES, 2, H * B, R), F32),
            pltpu.VMEM((EXCHANGES, 2, H * B, R), F32),
            pltpu.VMEM((2 * CSWEEPS, 2, HC * B, R), F32),
            pltpu.VMEM((2 * CSWEEPS, 2, HC * B, R), F32),
            pltpu.VMEM((2, H * B, rc * B), F32),
            pltpu.VMEM((2, H * B, rc * B), F32),
            dma((EXCHANGES, 2)),
            dma((EXCHANGES, 2)),
            dma((2, fan_size - 1)),
            dma((2, fan_size - 1)),
            dma((2 * CSWEEPS, 2)),
            dma((2 * CSWEEPS, 2)),
            dma((2,)),
            dma((2,)),
        ],
        compiler_params=pltpu.CompilerParams(
            collective_id=0, has_side_effects=True, vmem_limit_bytes=50 * 2**20),
    )(
        right_side.reshape(rows * B, R), fine_matrix, fine_columns, fine_inverse,
        prolong, aggregate, coarse_matrix, coarse_columns, coarse_inverse,
    )
    return solution_out.reshape(rows, B, R), residual_out.reshape(rows, B, R)


def solution(mesh):
    both = P(("coarse", "fan"))
    return jax.shard_map(
        functools.partial(body, mesh.shape["coarse"], mesh.shape["fan"]),
        mesh=mesh,
        in_specs=(both, both, both, both, both, both, P("coarse"), P("coarse"), P("coarse")),
        out_specs=(both, both),
        check_vma=False,
    )
```

```python
import functools

import jax
import jax.numpy as jnp
from jax import lax
from jax.experimental import pallas as pl
from jax.experimental.pallas import tpu as pltpu
from jax.sharding import PartitionSpec as P

H = 4
HC = 2
CSWEEPS = 4
EXCHANGES = 8
BATCHES = 1
relaxation = 0.6
MESH = pl.DeviceIdType.MESH
F32 = jnp.float32
BF16 = jnp.bfloat16


def dot(a, b):
    return jnp.dot(a, b, preferred_element_type=F32)


def two_term(matrix, halves):
    both = dot(matrix, halves)
    width = both.shape[1] // 2
    return both[:, :width] + both[:, width:]


def pack(value):
    n = value.shape[0] // BATCHES
    return jnp.concatenate([value[i * n:(i + 1) * n] for i in range(BATCHES)], axis=1)


def unpack(value):
    w = value.shape[1] // BATCHES
    return jnp.concatenate([value[:, i * w:(i + 1) * w] for i in range(BATCHES)], axis=0)


def kernel(
    coarse_size, fan_size,
    b_ref, a_ref, acol_ref, d_ref, p_ref, agg_ref, c_ref, ccol_ref, ci_ref,
    x_ref, res_ref,
    ad, dd, pd, ptd, cd, cid, bs, xs, xhl, ehl, e_ref, rhs, edge_out, halo_in,
    ce_out, ce_in, pe_out, pe_in,
    fs_sem, fr_sem, gs_sem, gr_sem, cs_sem, cr_sem, ps_sem, pr_sem,
):
    rows, slots, B, _ = a_ref.shape
    W = b_ref.shape[1] // BATCHES
    grows = c_ref.shape[0]
    rc = grows // fan_size
    HB = H * B
    CB = HC * B
    PB = rc * B
    ng = rows // H
    c = lax.axis_index("coarse")
    f = lax.axis_index("fan")
    place = c * fan_size + f
    before, after = place - 1, place + 1
    fine_to = (
        (before // fan_size, before % fan_size),
        (after // fan_size, after % fan_size),
    )
    fine_has = (place > 0, place < coarse_size * fan_size - 1)
    coarse_to = ((c - 1, f), (c + 1, f))
    coarse_has = (c > 0, c < coarse_size - 1)
    peers = [(c, (f + k) % fan_size) for k in range(1, fan_size)]

    barrier = pltpu.get_barrier_semaphore()
    for has, to in zip(fine_has + coarse_has, fine_to + coarse_to):
        @pl.when(has)
        def _():
            pl.semaphore_signal(barrier, inc=1, device_id=to, device_id_type=MESH)
    for to in peers:
        pl.semaphore_signal(barrier, inc=1, device_id=to, device_id_type=MESH)

    half = (lax.broadcasted_iota(jnp.int32, (1, 2 * B), 1) >= B).astype(jnp.int32)

    def build(count, blocks, names, pairs, dst):
        def row(r, carry):
            doubled = []
            for block in blocks(r):
                wide = block.astype(F32)
                doubled.append(jnp.concatenate([wide, wide], axis=1))
            named = names(r)
            for p in range(pairs):
                at = half + 2 * p
                total = None
                for block, name in zip(doubled, named):
                    term = jnp.where(at == name, block, 0.0)
                    total = term if total is None else total + term
                dst[pl.ds(pl.multiple_of(r * B, B), B), 2 * p * B:(2 * p + 2) * B] = total.astype(BF16)
            return carry

        lax.fori_loop(0, count, row, 0)

    def put_halves(ref, start, value):
        high = value.astype(BF16)
        low = (value - high.astype(F32)).astype(BF16)
        n = value.shape[0]
        ref[start:start + n, :W] = high
        ref[start:start + n, W:] = low

    def group(g):
        return slice(g * HB, (g + 1) * HB)

    cg = grows // H
    last = ng - 1

    def fine_copy(h, t, d):
        return pltpu.make_async_remote_copy(
            src_ref=edge_out.at[h, t, d], dst_ref=halo_in.at[h, t, 1 - d],
            send_sem=fs_sem.at[h, t, d], recv_sem=fr_sem.at[h, t, 1 - d],
            device_id=fine_to[d], device_id_type=MESH)

    def fine_send(h, t, d, value):
        edge_out[h, t, d] = pack(value)

        @pl.when(fine_has[d])
        def _():
            fine_copy(h, t, d).start()

    def fine_wait(h, t, d, slot):
        @pl.when(fine_has[d])
        def _():
            pltpu.make_async_remote_copy(
                src_ref=edge_out.at[h, t, 1 - d], dst_ref=halo_in.at[h, t, d],
                send_sem=fs_sem.at[h, t, 1 - d], recv_sem=fr_sem.at[h, t, d],
                device_id=fine_to[d], device_id_type=MESH).wait_recv()
            put_halves(xhl.at[h, slot], d * (rows + H) * B, unpack(halo_in[h, t, d]))

    def coarse_copy(h, s, d):
        return pltpu.make_async_remote_copy(
            src_ref=ce_out.at[h, s, d], dst_ref=ce_in.at[h, s, 1 - d],
            send_sem=cs_sem.at[h, s, d], recv_sem=cr_sem.at[h, s, 1 - d],
            device_id=coarse_to[d], device_id_type=MESH)

    def coarse_sent(d, final):
        if not final:
            return coarse_has[d]
        return coarse_has[d] & (f == (fan_size - 1 if d == 0 else 0))

    def coarse_came(d, final):
        if not final:
            return coarse_has[d]
        return coarse_has[d] & (f == (0 if d == 0 else fan_size - 1))

    def coarse_send(h, s, d, value, final):
        ce_out[h, s, d] = pack(value)

        @pl.when(coarse_sent(d, final))
        def _():
            coarse_copy(h, s, d).start()

    def coarse_wait(h, s, d, final):
        @pl.when(coarse_came(d, final))
        def _():
            pltpu.make_async_remote_copy(
                src_ref=ce_out.at[h, s, 1 - d], dst_ref=ce_in.at[h, s, d],
                send_sem=cs_sem.at[h, s, 1 - d], recv_sem=cr_sem.at[h, s, d],
                device_id=coarse_to[d], device_id_type=MESH).wait_recv()
            put_halves(ehl.at[h], d * (grows + HC) * B, unpack(ce_in[h, s, d]))

    def edge_matrix_copy(d):
        return pltpu.make_async_remote_copy(
            src_ref=pe_out.at[d], dst_ref=pe_in.at[1 - d],
            send_sem=ps_sem.at[d], recv_sem=pr_sem.at[1 - d],
            device_id=fine_to[d], device_id_type=MESH)

    def gather_copy(h, cycle, k, piece):
        return pltpu.make_async_remote_copy(
            src_ref=rhs.at[h, cycle, piece], dst_ref=rhs.at[h, cycle, piece],
            send_sem=gs_sem.at[h, cycle, k], recv_sem=gr_sem.at[h, cycle, k],
            device_id=peers[k], device_id_type=MESH)

    def step_of(g, residual):
        return relaxation * dot(dd[group(g), :], residual.astype(BF16))

    def set_group(h, g, value, slot, t):
        if t is not None and g == 0:
            fine_send(h, t, 0, value)
        if t is not None and g == last:
            fine_send(h, t, 1, value)
        xs[h, group(g), :] = value
        put_halves(xhl.at[h, slot], (g + 1) * HB, value)

    def residuals(h, slot, t, use):
        def edges():
            low = bs[h, group(0), :] - two_term(ad[group(0), HB:], xhl[h, slot, HB:3 * HB, :])
            high = bs[h, group(last), :] - two_term(
                ad[group(last), :2 * HB], xhl[h, slot, last * HB:(last + 2) * HB, :])
            return low, high

        def inner():
            for g in range(1, ng - 1):
                use(g, bs[h, group(g), :] - two_term(
                    ad[group(g), :], xhl[h, slot, g * HB:(g + 3) * HB, :]))

        if t is None:
            low, high = edges()
        else:
            inner()
            low, high = edges()
            yield
            fine_wait(h, t, 0, slot)
        use(0, low - two_term(ad[group(0), :HB], xhl[h, slot, :HB, :]))
        if t is not None:
            fine_wait(h, t, 1, slot)
        use(last, high - two_term(
            ad[group(last), 2 * HB:], xhl[h, slot, (last + 2) * HB:, :]))
        if t is None:
            inner()

    def sweep(h, slot, t_in, t_out):
        def use(g, residual):
            set_group(h, g, xs[h, group(g), :] + step_of(g, residual), 1 - slot, t_out)

        yield from residuals(h, slot, t_in, use)

    def relax_coarse(values):
        return [
            relaxation * dot(cid[group(g), :], v.astype(BF16)) for g, v in enumerate(values)
        ]

    def build_prolong():
        build(rows, lambda r: [p_ref[r]], lambda r: [agg_ref[r]], rc // 2, pd)
        for g in range(ng):
            ptd[:, group(g)] = jnp.transpose(pd[group(g), :].astype(F32)).astype(BF16)

    def build_coarse():
        build(
            grows,
            lambda r: [c_ref[r, k] for k in range(c_ref.shape[1])],
            lambda r: [ccol_ref[r, k] for k in range(c_ref.shape[1])],
            (grows + 2 * HC) // 2, cd)
        build(grows, lambda r: [ci_ref[r]], lambda r: [r % H], H // 2, cid)

    def correct(h, cycle, slot, t_in):
        pieces = []
        if cycle == 0 and h == 0:
            build_prolong()

        def use(g, residual):
            pieces.append(dot(ptd[:, group(g)], residual.astype(BF16)))

        yield from residuals(h, slot, t_in, use)
        rhs[h, cycle, f] = pack(functools.reduce(jnp.add, pieces))
        for k in range(fan_size - 1):
            gather_copy(h, cycle, k, f).start()
        if cycle == 0 and h == BATCHES - 1:
            pe_out[0] = pd[:HB, :].astype(F32)
            pe_out[1] = pd[last * HB:, :].astype(F32)
            for d in range(2):
                @pl.when(fine_has[d])
                def _():
                    edge_matrix_copy(d).start()
            build_coarse()
        yield
        for k in range(fan_size - 1):
            gather_copy(h, cycle, k, (f + 2 * fan_size - k - 1) % fan_size).wait_recv()
        whole = [unpack(rhs[h, cycle, i]) for i in range(fan_size)]
        whole = jnp.concatenate(whole, axis=0)
        whole = [whole[group(g)] for g in range(cg)]
        own_rows = slice(CB, CB + grows * B)

        def publish(e, s, final):
            coarse_send(h, s, 0, e[0][:CB, :], final)
            coarse_send(h, s, 1, e[-1][HB - CB:, :], final)
            for g in range(cg):
                e_ref[h, group(g), :] = e[g]
                put_halves(ehl.at[h], CB + g * HB, e[g])

        s = cycle * CSWEEPS
        publish(relax_coarse(whole), s, False)
        for step in range(1, CSWEEPS):
            own = [
                whole[g] - two_term(cd[group(g), own_rows], ehl[h, own_rows, :])
                for g in range(cg)
            ]
            yield
            coarse_wait(h, s, 0, False)
            coarse_wait(h, s, 1, False)
            own = [v - two_term(cd[group(g), :CB], ehl[h, :CB, :]) for g, v in enumerate(own)]
            own = [
                v - two_term(cd[group(g), CB + grows * B:], ehl[h, CB + grows * B:, :])
                for g, v in enumerate(own)
            ]
            e = [e_ref[h, group(g), :] + v for g, v in enumerate(relax_coarse(own))]
            s = s + 1
            publish(e, s, step == CSWEEPS - 1)

        other = 1 - slot
        lifted = ehl[h, pl.ds(pl.multiple_of(CB + f * PB, PB), PB), :]
        for g in range(ng):
            set_group(h, g, xs[h, group(g), :] + two_term(pd[group(g), :], lifted), other, None)
        yield
        for d in range(2):
            if cycle == 0 and h == 0:
                @pl.when(fine_has[d])
                def _():
                    pltpu.make_async_remote_copy(
                        src_ref=pe_out.at[1 - d], dst_ref=pe_in.at[d],
                        send_sem=ps_sem.at[1 - d], recv_sem=pr_sem.at[d],
                        device_id=fine_to[d], device_id_type=MESH).wait_recv()
            coarse_wait(h, s, d, True)

            @pl.when(fine_has[d])
            def _():
                theirs = ehl[h, pl.ds(pl.multiple_of(CB + (f + 2 * d - 1) * PB, PB), PB), :]
                value = unpack(halo_in[h, t_in, d]) + two_term(pe_in[d].astype(BF16), theirs)
                put_halves(xhl.at[h, other], d * (rows + H) * B, value)

    build(rows, lambda r: [d_ref[r]], lambda r: [r % H], H // 2, dd)
    waits = (
        sum(h.astype(jnp.int32) for h in fine_has + coarse_has) + (fan_size - 1)
    )
    pl.semaphore_wait(barrier, waits)
    for h in range(BATCHES):
        bs[h] = b_ref[:, h * W:(h + 1) * W]
        for g in (0, last):
            set_group(h, g, step_of(g, bs[h, group(g), :]), 0, 0)
    for h in range(BATCHES):
        for g in range(1, last):
            set_group(h, g, step_of(g, bs[h, group(g), :]), 0, 0)
    for d in range(2):
        @pl.when(jnp.logical_not(fine_has[d]))
        def _():
            at = d * (rows + H) * B
            for h in range(BATCHES):
                for slot in range(2):
                    xhl[h, slot, at:at + HB, :] = jnp.zeros((HB, 2 * W), BF16)

        @pl.when(jnp.logical_not(coarse_has[d]))
        def _():
            at = d * (grows + HC) * B
            for h in range(BATCHES):
                ehl[h, at:at + CB, :] = jnp.zeros((CB, 2 * W), BF16)

    build(
        rows,
        lambda r: [a_ref[r, k] for k in range(slots)],
        lambda r: [acol_ref[r, k] - (r // H) * H for k in range(slots)],
        3 * H // 2, ad)

    def batch(h):
        def keep(g, residual):
            res_ref[group(g), h * W:(h + 1) * W] = residual

        yield from sweep(h, 0, 0, 1)
        yield from correct(h, 0, 1, 1)
        yield from sweep(h, 0, None, 2)
        yield from sweep(h, 1, 2, 3)
        yield from sweep(h, 0, 3, 4)
        yield from sweep(h, 1, 4, 5)
        yield from correct(h, 1, 0, 5)
        yield from sweep(h, 1, None, 6)
        yield from sweep(h, 0, 6, 7)
        x_ref[:, h * W:(h + 1) * W] = xs[h]
        yield from residuals(h, 1, 7, keep)

    running = [batch(h) for h in range(BATCHES)]
    while running:
        running = [one for one in running if next(one, running) is not running]

    for h in range(BATCHES):
        for cycle in range(2):
            for k in range(fan_size - 1):
                gather_copy(h, cycle, k, f).wait_send()
    for d in range(2):
        @pl.when(fine_has[d])
        def _():
            for h in range(BATCHES):
                for t in range(EXCHANGES):
                    fine_copy(h, t, d).wait_send()
            edge_matrix_copy(d).wait_send()

        for s in range(2 * CSWEEPS):
            @pl.when(coarse_sent(d, s % CSWEEPS == CSWEEPS - 1))
            def _():
                for h in range(BATCHES):
                    coarse_copy(h, s, d).wait_send()


def body(coarse_size, fan_size, right_side, fine_matrix, fine_columns, fine_inverse,
         prolong, aggregate, coarse_matrix, coarse_columns, coarse_inverse):
    rows, B, R = right_side.shape
    grows = coarse_matrix.shape[0]
    rc = grows // fan_size
    W = R // BATCHES
    vmem = pl.BlockSpec(memory_space=pltpu.VMEM)
    smem = pl.BlockSpec(memory_space=pltpu.SMEM)
    flat = jax.ShapeDtypeStruct((rows * B, R), F32)
    dma = pltpu.SemaphoreType.DMA
    solution_out, residual_out = pl.pallas_call(
        functools.partial(kernel, coarse_size, fan_size),
        out_shape=(flat, flat),
        in_specs=[vmem, vmem, smem, vmem, vmem, smem, vmem, smem, vmem],
        out_specs=(vmem, vmem),
        scratch_shapes=[
            pltpu.VMEM((rows * B, 3 * H * B), BF16),
            pltpu.VMEM((rows * B, H * B), BF16),
            pltpu.VMEM((rows * B, rc * B), BF16),
            pltpu.VMEM((rc * B, rows * B), BF16),
            pltpu.VMEM((grows * B, (grows + 2 * HC) * B), BF16),
            pltpu.VMEM((grows * B, H * B), BF16),
            pltpu.VMEM((BATCHES, rows * B, W), F32),
            pltpu.VMEM((BATCHES, rows * B, W), F32),
            pltpu.VMEM((BATCHES, 2, (rows + 2 * H) * B, 2 * W), BF16),
            pltpu.VMEM((BATCHES, (grows + 2 * HC) * B, 2 * W), BF16),
            pltpu.VMEM((BATCHES, grows * B, W), F32),
            pltpu.VMEM((BATCHES, 2, fan_size, rc * B // BATCHES, R), F32),
            pltpu.VMEM((BATCHES, EXCHANGES, 2, H * B // BATCHES, R), F32),
            pltpu.VMEM((BATCHES, EXCHANGES, 2, H * B // BATCHES, R), F32),
            pltpu.VMEM((BATCHES, 2 * CSWEEPS, 2, HC * B // BATCHES, R), F32),
            pltpu.VMEM((BATCHES, 2 * CSWEEPS, 2, HC * B // BATCHES, R), F32),
            pltpu.VMEM((2, H * B, rc * B), F32),
            pltpu.VMEM((2, H * B, rc * B), F32),
            dma((BATCHES, EXCHANGES, 2)),
            dma((BATCHES, EXCHANGES, 2)),
            dma((BATCHES, 2, fan_size - 1)),
            dma((BATCHES, 2, fan_size - 1)),
            dma((BATCHES, 2 * CSWEEPS, 2)),
            dma((BATCHES, 2 * CSWEEPS, 2)),
            dma((2,)),
            dma((2,)),
        ],
        compiler_params=pltpu.CompilerParams(
            collective_id=0, has_side_effects=True, vmem_limit_bytes=50 * 2**20),
    )(
        right_side.reshape(rows * B, R), fine_matrix, fine_columns, fine_inverse,
        prolong, aggregate, coarse_matrix, coarse_columns, coarse_inverse,
    )
    return solution_out.reshape(rows, B, R), residual_out.reshape(rows, B, R)


def solution(mesh):
    both = P(("coarse", "fan"))
    return jax.shard_map(
        functools.partial(body, mesh.shape["coarse"], mesh.shape["fan"]),
        mesh=mesh,
        in_specs=(both, both, both, both, both, both, P("coarse"), P("coarse"), P("coarse")),
        out_specs=(both, both),
        check_vma=False,
    )
```
